32 devices in a mesh: parts: 2 (over x), store: 8 (over z, y), query: 2 (over core).
Axes of the slice: x: 2, y: 2, z: 4, core: 2. Of those that a mesh axis runs over, the one named last changes fastest.
Arguments:
- queries: bfloat16 [16, 768, 1024], P(('parts', 'store'), 'query'), parts along dimension 0, may hold values from -6 to 6
- store_blocks: bfloat16 [512, 128, 1024], P(('parts', 'store')), parts along dimension 0, may hold values from -6 to 6
- cand_owner: int32 [16, 112], P(('parts', 'store'), 'query'), parts along dimension 0, may hold values from 0 to 7, as said below
- cand_block: int32 [16, 112], P(('parts', 'store'), 'query'), parts along dimension 0, may hold values from 0 to 31
- pattern: int32 [16, 112, 6], P(('parts', 'store'), 'query'), parts along dimension 0, may hold values 0 or 1
- slot_index: int32 [16, 112], P(('parts', 'store'), 'query'), parts along dimension 0, may hold values from 0 to 31
Outputs:
- result: float32 [16, 32, 768], P(('parts', 'store'), None, 'query'), parts along dimension 0
The draws below stay inside these ranges and needn't reach their ends.
There are 2 independent parts, one for each index of `parts`. The reference program is written for one: setup_inputs(seed, part) draws one part's arguments, and reference() takes and returns one part's arrays. A program takes and returns all parts, laid end to end along the dimension named above; each array names one. Nothing has to cross between parts.
Inputs may be any that keep to these rules, and one draw needn't show every extreme that they name: `cand_owner`: each tile's candidate list is 2 runs of 56 entries in order. Within one run no storage shard appears more than 10 times, and one shard appears exactly 10 times.
All inputs are finite; a program needn't handle non-finite values. No bound on the sum of `pattern` on one device may be relied on, other than what follows from the above.
Results may differ from the reference program's by a relative error of at most 0.0003.
Values may be sent and summed in bfloat16 or wider, within the bound.
A program may use at most 128 MiB of HBM per device.

```python
import math
import jax
import jax.numpy as jnp
from jax import lax

D = 1024
BLOCK = 128
SUB = 128
SLOTS = 32
QT = 768
CAND_DEV = 56
BLK_DEV = 32
TILES = 8
CAND = 112
NSUB = 6
CAP = 10
STORED = 256


def draw_cand_owner(key, part):
    key = jax.random.fold_in(key, 7)
    segments = TILES * (CAND // CAND_DEV)
    subkeys = jax.random.split(key, segments)

    def one_list(subkey):
        hottest = jax.random.randint(jax.random.fold_in(subkey, 1), (), 0, TILES).astype(jnp.int32)
        reserve = (hottest + 1 + jnp.arange((TILES - 1) * CAP, dtype=jnp.int32) // CAP) % TILES
        others = jax.random.permutation(jax.random.fold_in(subkey, 2), reserve)[:CAND_DEV - CAP]
        full_list = jnp.concatenate([jnp.full((CAP,), hottest, jnp.int32), others.astype(jnp.int32)])
        return jax.random.permutation(jax.random.fold_in(subkey, 3), full_list)
    owner_lists = jax.vmap(one_list)(subkeys)
    return owner_lists.reshape(TILES, CAND).astype(jnp.int32)


def touch_ends(array, rng, smallest, largest):
    place = [jax.random.randint(jax.random.fold_in(rng, axis), (), 0, length) for axis, length in enumerate(array.shape)]
    widest = array.shape.index(max(array.shape))
    neighbour = place[:widest] + [(place[widest] + 1) % array.shape[widest]] + place[widest + 1:]
    return array.at[tuple(place)].set(smallest).at[tuple(neighbour)].set(largest)


def block_levels(stream_key, shape, cuts, smallest, high):
    def one(dim, shards_of):
        heights = jax.random.uniform(jax.random.fold_in(jax.random.fold_in(stream_key, 6), dim), (shards_of,), jnp.float32, smallest / len(cuts), high / len(cuts))
        return jnp.repeat(jnp.exp(heights), shape[dim] // shards_of).reshape((-1,) + (1,) * (len(shape) - dim - 1))

    factor_of = one(*cuts[0])
    for cut in cuts[1:]:
        factor_of = factor_of * one(*cut)
    return factor_of


def normal_values(key, extent, deviation, reach, cuts=(), kind=jnp.bfloat16):
    result = deviation * jax.random.normal(key, extent, jnp.float32)
    if cuts:
        result = result * block_levels(key, extent, cuts, -0.22, 0.18)
    return jnp.clip(result, -reach, reach).astype(kind)


def setup_inputs(seed: int = 0, part: int = 0) -> dict:
    seeds = jax.random.split(jax.random.key(seed), 7)
    own_keys = jax.random.split(jax.random.fold_in(seeds[6], part), 7)
    queries = normal_values(own_keys[0], (TILES, QT, D), 1.0, 6.0, ((0, 8), (1, 2)))
    store_blocks = normal_values(own_keys[1], (STORED, BLOCK, D), 1.0, 6.0, ((0, 8),))
    cand_owner = draw_cand_owner(jax.random.fold_in(jax.random.fold_in(seeds[6], part), 71), part)
    cand_block = touch_ends(jax.random.randint(own_keys[3], (TILES, CAND), 0, BLK_DEV), jax.random.fold_in(own_keys[3], 1), 0, BLK_DEV - 1).astype(jnp.int32)
    pattern = touch_ends((jax.random.randint(own_keys[4], (TILES, CAND, NSUB), 0, 2) < 1).astype(jnp.int32), jax.random.fold_in(own_keys[4], 1), 0, 1)
    slot_index = touch_ends(jax.random.randint(own_keys[5], (TILES, CAND), 0, SLOTS), jax.random.fold_in(own_keys[5], 1), 0, SLOTS - 1).astype(jnp.int32)
    return {"queries": queries, "store_blocks": store_blocks, "cand_owner": cand_owner, "cand_block": cand_block, "pattern": pattern, "slot_index": slot_index}


def tile_maxima(whole_tile, owner_list, local_list, mask_rows, slot_list, store_blocks):
    stored_rows = owner_list * BLK_DEV + local_list
    blocks = store_blocks[stored_rows]
    widened = blocks.astype(jnp.float32)
    squares = lax.optimization_barrier(jnp.mean(widened * widened, axis=-1))
    inverse = lax.rsqrt(squares + 1e-06) * (1.0 / math.sqrt(D))
    products = jnp.einsum('qd,cvd->cqv', whole_tile.astype(jnp.float32), widened)
    best_scores = lax.optimization_barrier(jnp.max(products * inverse[:, None, :], axis=-1))
    live_mask = jnp.repeat(mask_rows, SUB, axis=1) == 1
    slot_match = slot_list[:, None] == jnp.arange(SLOTS, dtype=jnp.int32)[None, :]
    masked = jnp.where(live_mask[:, None, :] & slot_match[:, :, None], best_scores[:, None, :], jnp.float32(0.0))
    return lax.optimization_barrier(jnp.max(masked, axis=0))

def reference(queries, store_blocks, cand_owner, cand_block, pattern, slot_index):

    def one_tile(items):
        return tile_maxima(items[0], items[1], items[2], items[3], items[4], store_blocks)
    return lax.map(one_tile, (queries, cand_owner, cand_block, pattern, slot_index))
```

```python
import functools
import math

import jax
import jax.numpy as jnp
from jax import lax
from jax.experimental import pallas as pl
from jax.experimental.pallas import tpu as pltpu
from jax.sharding import PartitionSpec as P

SUB = 128
SLOTS = 32
MIB = 1024 * 1024


def chunk_list(rows):
    last = rows // 6
    parts = [rows // 6, rows // 3, rows // 3, last]
    chunks, start = [], 0
    for size in parts:
        chunks.append((start, size))
        start += size
    assert start == rows
    return chunks


def kernel(
    n,
    group,
    q_hbm,
    blocks_hbm,
    owner_hbm,
    block_hbm,
    pattern_hbm,
    slot_hbm,
    out_ref,
    blocks,
    gathered,
    scale,
    best_out,
    best_in,
    owner_v,
    block_v,
    pattern_v,
    slot_v,
    owner_s,
    block_s,
    pattern_s,
    slot_s,
    local_sem,
    recv_sem,
    send_sem,
    best_recv,
    best_send,
    meta_recv,
    meta_send,
    smem_sem,
):
    ny = 2
    nz = n // ny
    rows = gathered.shape[1]
    stored, width, depth = blocks.shape
    chunks = chunk_list(rows)
    last = len(chunks) - 1
    me = lax.axis_index("store")
    core = lax.axis_index("query")
    y = lax.rem(me, ny)
    z = me // ny
    other_y = 1 - y
    UP, DOWN, ACROSS = 0, 1, 2

    load_blocks = pltpu.make_async_copy(blocks_hbm, blocks, local_sem.at[0])
    load_blocks.start()
    load_own = pltpu.make_async_copy(q_hbm.at[0], gathered.at[me], local_sem.at[1])
    load_own.start()

    barrier = pltpu.get_barrier_semaphore()

    @pl.loop(1, n)
    def _(step):
        pl.semaphore_signal(barrier, inc=1, device_id={"store": lax.rem(me + step, n)})

    pl.semaphore_signal(barrier, inc=1, device_id={"query": 1 - core})
    pl.semaphore_wait(barrier, n)

    targets = (
        jnp.minimum(z + 1, nz - 1) * ny + y,
        jnp.maximum(z - 1, 0) * ny + y,
        z * ny + other_y,
    )

    def copy_of(tile, c, way, own=False):
        start, size = chunks[c]
        held = gathered.at[tile, pl.ds(start, size)]
        return pltpu.make_async_remote_copy(
            src_ref=q_hbm.at[0, pl.ds(start, size)] if own else held,
            dst_ref=held,
            send_sem=send_sem.at[way, tile, c],
            recv_sem=recv_sem.at[tile, c],
            device_id={"store": targets[way]},
        )

    def wait_chunk(tile, c):
        copy_of(tile, c, ACROSS).wait_recv()

    for c in [last] + list(range(last)):
        copy_of(me, c, ACROSS, True).start()
    for c in range(last + 1):
        @pl.when(z > 0)
        def _():
            copy_of(me, c, DOWN, True).start()

        @pl.when(z < nz - 1)
        def _():
            copy_of(me, c, UP, True).start()

    metas = [
        pltpu.make_async_remote_copy(
            src_ref=src,
            dst_ref=dst,
            send_sem=meta_send.at[i],
            recv_sem=meta_recv.at[i],
            device_id={"query": 1 - core},
        )
        for i, (src, dst) in enumerate(
            [(owner_hbm, owner_v), (block_hbm, block_v), (pattern_hbm, pattern_v), (slot_hbm, slot_v)]
        )
    ]
    for copy in metas:
        copy.start()
    own_meta = [
        pltpu.make_async_copy(src, dst.at[0], smem_sem.at[i])
        for i, (src, dst) in enumerate(
            [(owner_hbm, owner_s), (block_hbm, block_s), (pattern_hbm, pattern_s), (slot_hbm, slot_s)]
        )
    ]
    for copy in own_meta:
        copy.start()

    load_blocks.wait()

    @pl.loop(0, stored)
    def _(b):
        wide = blocks[b].astype(jnp.float32)
        mean = jnp.sum(wide * wide, axis=1, keepdims=True) * (1.0 / depth)
        inverse = lax.rsqrt(mean + 1e-06) * (1.0 / math.sqrt(depth))
        scale[b] = jnp.broadcast_to(inverse, (width, SUB))

    def best_copy(tile):
        return pltpu.make_async_remote_copy(
            src_ref=best_out.at[tile],
            dst_ref=best_in.at[pl.ds(pl.multiple_of(me * stored, stored), stored)],
            send_sem=best_send.at[tile],
            recv_sem=best_recv.at[me],
            device_id={"store": tile},
        )

    def score(tile):
        @pl.loop(0, stored // group)
        def _(g):
            first = pl.multiple_of(g * group, group)
            picked = blocks[pl.ds(first, group)].reshape(group * width, depth)
            products = lax.dot_general(
                picked,
                gathered[tile],
                (((1,), (1,)), ((), ())),
                preferred_element_type=jnp.float32,
            ).reshape(group, width, rows)
            factor = scale[pl.ds(first, group)]
            for j in range(rows // SUB):
                piece = products[:, :, j * SUB : (j + 1) * SUB] * factor
                best_out[tile, pl.ds(first, group), j * SUB : (j + 1) * SUB] = jnp.max(piece, axis=1)

    def score_and_send(tile):
        score(tile)
        best_copy(tile).start()

    load_own.wait()
    score(me)
    best_in[pl.ds(pl.multiple_of(me * stored, stored), stored), :] = best_out[me]

    def pass_second(distance):
        above, below = z + distance, z - distance

        @pl.when(above < nz)
        def _():
            tile = above * ny + other_y
            wait_chunk(tile, last)

            @pl.when(z > 0)
            def _():
                copy_of(tile, last, DOWN).start()

        @pl.when(below >= 0)
        def _():
            tile = below * ny + other_y
            wait_chunk(tile, last)

            @pl.when(z < nz - 1)
            def _():
                copy_of(tile, last, UP).start()

    def finish_across(distance):
        for side in (1, -1):
            place = z + side * distance

            @pl.when((place >= 0) & (place < nz))
            def _():
                tile = place * ny + other_y
                for c in range(last):
                    wait_chunk(tile, c)
                score_and_send(tile)

    def pass_line(distance):
        above, below = z + distance, z - distance
        for c in range(last + 1):
            @pl.when(above < nz)
            def _():
                tile = above * ny + y
                wait_chunk(tile, c)

                @pl.when(z > 0)
                def _():
                    copy_of(tile, c, DOWN).start()

                if c < last:
                    copy_of(tile, c, ACROSS).start()

            @pl.when(below >= 0)
            def _():
                tile = below * ny + y
                wait_chunk(tile, c)

                @pl.when(z < nz - 1)
                def _():
                    copy_of(tile, c, UP).start()

                if c < last:
                    copy_of(tile, c, ACROSS).start()

    def score_line(distance):
        for side in (1, -1):
            place = z + side * distance

            @pl.when((place >= 0) & (place < nz))
            def _():
                score_and_send(place * ny + y)

    own_other = z * ny + other_y
    wait_chunk(own_other, last)

    @pl.when(z > 0)
    def _():
        copy_of(own_other, last, DOWN).start()

    @pl.when(z < nz - 1)
    def _():
        copy_of(own_other, last, UP).start()

    for c in range(last):
        wait_chunk(own_other, c)
    score_and_send(own_other)

    @pl.loop(1, nz)
    def _(distance):
        pass_line(distance)
        pass_second(distance)

        @pl.when(distance > 1)
        def _():
            finish_across(distance - 1)

        score_line(distance)

    finish_across(nz - 1)

    for copy in metas:
        copy.wait()
    for copy in own_meta:
        copy.wait()
    other_meta = [
        pltpu.make_async_copy(src, dst.at[1], smem_sem.at[i])
        for i, (src, dst) in enumerate(
            [(owner_v, owner_s), (block_v, block_s), (pattern_v, pattern_s), (slot_v, slot_s)]
        )
    ]
    for copy in other_meta:
        copy.start()
    for copy in other_meta:
        copy.wait()

    @pl.loop(1, n)
    def _(step):
        source = lax.rem(me + step, n)
        pltpu.make_async_remote_copy(
            src_ref=best_out.at[source],
            dst_ref=best_in.at[pl.ds(pl.multiple_of(source * stored, stored), stored)],
            send_sem=best_send.at[source],
            recv_sem=best_recv.at[source],
            device_id={"store": source},
        ).wait_recv()

    length = owner_s.shape[2]
    subs = rows // SUB
    slots = lax.broadcasted_iota(jnp.int32, (SLOTS, SUB), 0)

    def merge(c, totals):
        totals = list(totals)
        for run in range(2):
            source = owner_s[run, 0, c] * stored + block_s[run, 0, c]
            row = best_in[pl.ds(source, 1), :]
            slot = slot_s[run, 0, c]
            for j in range(subs):
                live = pattern_s[run, 0, c, core * subs + j] == 1
                wanted = jnp.where(live, slot, -1)
                piece = jnp.broadcast_to(row[:, j * SUB : (j + 1) * SUB], (SLOTS, SUB))
                totals[j] = jnp.maximum(totals[j], jnp.where(slots == wanted, piece, 0.0))
        return tuple(totals)

    zero = jnp.zeros((SLOTS, SUB), jnp.float32)
    totals = lax.fori_loop(0, length, merge, (zero,) * subs)
    for j in range(subs):
        out_ref[0, :, j * SUB : (j + 1) * SUB] = totals[j]

    for c in range(last + 1):
        copy_of(me, c, ACROSS, True).wait_send()

    @pl.loop(0, nz)
    def _(place):
        tile = place * ny + y
        across = place * ny + other_y

        @pl.when(place != z)
        def _():
            for c in range(last):
                copy_of(tile, c, ACROSS).wait_send()

        @pl.when((place <= z) & (z < nz - 1))
        def _():
            for c in range(last + 1):
                copy_of(tile, c, UP).wait_send()
            copy_of(across, last, UP).wait_send()

        @pl.when((place >= z) & (z > 0))
        def _():
            for c in range(last + 1):
                copy_of(tile, c, DOWN).wait_send()
            copy_of(across, last, DOWN).wait_send()

    @pl.loop(1, n)
    def _(step):
        best_copy(lax.rem(me + step, n)).wait_send()


def body(queries, store_blocks, cand_owner, cand_block, pattern, slot_index):
    n = lax.axis_size("store")
    rows, depth = queries.shape[1:]
    stored, width = store_blocks.shape[:2]
    length, subs = pattern.shape[1:]
    chunk_count = len(chunk_list(rows))
    flat = (1, length)
    return pl.pallas_call(
        functools.partial(kernel, n, 8),
        out_shape=jax.ShapeDtypeStruct((1, SLOTS, rows), jnp.float32),
        in_specs=[pl.BlockSpec(memory_space=pl.ANY)] * 6,
        out_specs=pl.BlockSpec(memory_space=pltpu.VMEM),
        scratch_shapes=[
            pltpu.VMEM((stored, width, depth), jnp.bfloat16),
            pltpu.VMEM((n, rows, depth), jnp.bfloat16),
            pltpu.VMEM((stored, width, SUB), jnp.float32),
            pltpu.VMEM((n, stored, rows), jnp.float32),
            pltpu.VMEM((n * stored, rows), jnp.float32),
            pltpu.VMEM(flat, jnp.int32),
            pltpu.VMEM(flat, jnp.int32),
            pltpu.VMEM((1, length, subs), jnp.int32),
            pltpu.VMEM(flat, jnp.int32),
            pltpu.SMEM((2,) + flat, jnp.int32),
            pltpu.SMEM((2,) + flat, jnp.int32),
            pltpu.SMEM((2, 1, length, subs), jnp.int32),
            pltpu.SMEM((2,) + flat, jnp.int32),
            pltpu.SemaphoreType.DMA((2,)),
            pltpu.SemaphoreType.DMA((n, chunk_count)),
            pltpu.SemaphoreType.DMA((3, n, chunk_count)),
            pltpu.SemaphoreType.DMA((n,)),
            pltpu.SemaphoreType.DMA((n,)),
            pltpu.SemaphoreType.DMA((4,)),
            pltpu.SemaphoreType.DMA((4,)),
            pltpu.SemaphoreType.DMA((4,)),
        ],
        compiler_params=pltpu.CompilerParams(
            collective_id=0, has_side_effects=True, vmem_limit_bytes=52 * MIB
        ),
        cost_estimate=pl.CostEstimate(
            flops=2 * n * rows * stored * width * depth,
            bytes_accessed=stored * width * depth * 2,
            transcendentals=0,
        ),
    )(queries, store_blocks, cand_owner, cand_block, pattern, slot_index)


def solution(mesh):
    placed = (
        P(("parts", "store"), "query", None),
        P(("parts", "store"), None, None),
        P(("parts", "store"), "query"),
        P(("parts", "store"), "query"),
        P(("parts", "store"), "query", None),
        P(("parts", "store"), "query"),
    )
    return jax.shard_map(
        body,
        mesh=mesh,
        in_specs=placed,
        out_specs=P(("parts", "store"), None, "query"),
        check_vma=False,
    )
```

```python
import functools
import math

import jax
import jax.numpy as jnp
from jax import lax
from jax.experimental import pallas as pl
from jax.experimental.pallas import tpu as pltpu
from jax.sharding import PartitionSpec as P

SUB = 128
SLOTS = 32
MIB = 1024 * 1024


CHUNKS = 6
UNIT = 256


def kernel(
    n,
    group,
    q_hbm,
    blocks_hbm,
    owner_hbm,
    block_hbm,
    pattern_hbm,
    slot_hbm,
    out_ref,
    blocks,
    gathered,
    scale,
    best_out,
    best_in,
    owner_v,
    block_v,
    pattern_v,
    slot_v,
    owner_s,
    block_s,
    pattern_s,
    slot_s,
    local_sem,
    recv_sem,
    send_sem,
    best_recv,
    best_send,
    meta_recv,
    meta_send,
    smem_sem,
):
    ny = 2
    nz = n // ny
    rows = gathered.shape[0] // n
    piece_rows = rows // CHUNKS
    subs = rows // SUB
    stored, width, depth = blocks.shape
    last = CHUNKS - 1
    me = lax.axis_index("store")
    core = lax.axis_index("query")
    y = lax.rem(me, ny)
    z = me // ny
    other_y = 1 - y
    UP, DOWN, ACROSS = 0, 1, 2
    mine = z * ny

    def rows_of(slot, c, count=1):
        start = pl.multiple_of(slot * rows + c * piece_rows, piece_rows)
        return gathered.at[pl.ds(start, count * piece_rows)]

    load_blocks = pltpu.make_async_copy(blocks_hbm, blocks, local_sem.at[0])
    load_blocks.start()
    load_own = pltpu.make_async_copy(q_hbm.at[0], rows_of(mine, 0, CHUNKS), local_sem.at[1])
    load_own.start()

    barrier = pltpu.get_barrier_semaphore()

    @pl.loop(1, n)
    def _(step):
        pl.semaphore_signal(barrier, inc=1, device_id={"store": lax.rem(me + step, n)})

    pl.semaphore_signal(barrier, inc=1, device_id={"query": 1 - core})
    pl.semaphore_wait(barrier, n)

    targets = (
        jnp.minimum(z + 1, nz - 1) * ny + y,
        jnp.maximum(z - 1, 0) * ny + y,
        z * ny + other_y,
    )

    def copy_of(slot, c, way, own=False):
        source = q_hbm.at[0, pl.ds(c * piece_rows, piece_rows)] if own else rows_of(slot, c)
        landing = slot + 1 if way == ACROSS else slot
        return pltpu.make_async_remote_copy(
            src_ref=source,
            dst_ref=rows_of(landing, c),
            send_sem=send_sem.at[way, slot, c],
            recv_sem=recv_sem.at[landing, c],
            device_id={"store": targets[way]},
        )

    def wait_chunk(slot, c):
        copy_of(slot, c, UP).wait_recv()

    for c in [last] + list(range(last)):
        copy_of(mine, c, ACROSS, True).start()
    for c in range(last + 1):
        @pl.when(z > 0)
        def _():
            copy_of(mine, c, DOWN, True).start()

        @pl.when(z < nz - 1)
        def _():
            copy_of(mine, c, UP, True).start()

    metas = [
        pltpu.make_async_remote_copy(
            src_ref=src,
            dst_ref=dst,
            send_sem=meta_send.at[i],
            recv_sem=meta_recv.at[i],
            device_id={"query": 1 - core},
        )
        for i, (src, dst) in enumerate(
            [(owner_hbm, owner_v), (block_hbm, block_v), (pattern_hbm, pattern_v), (slot_hbm, slot_v)]
        )
    ]
    for copy in metas:
        copy.start()
    own_meta = [
        pltpu.make_async_copy(src, dst.at[0], smem_sem.at[i])
        for i, (src, dst) in enumerate(
            [(owner_hbm, owner_s), (block_hbm, block_s), (pattern_hbm, pattern_s), (slot_hbm, slot_s)]
        )
    ]
    for copy in own_meta:
        copy.start()

    load_blocks.wait()

    @pl.loop(0, stored)
    def _(b):
        wide = blocks[b].astype(jnp.float32)
        mean = jnp.sum(wide * wide, axis=1, keepdims=True) * (1.0 / depth)
        inverse = lax.rsqrt(mean + 1e-06) * (1.0 / math.sqrt(depth))
        scale[b] = jnp.broadcast_to(inverse, (width, SUB))

    def best_copy(slot, first, count):
        tile = (slot // ny) * ny + lax.rem(slot + y, ny)
        return pltpu.make_async_remote_copy(
            src_ref=best_out.at[pl.ds(slot * subs + first, count)],
            dst_ref=best_in.at[pl.ds(me * subs + first, count)],
            send_sem=best_send.at[slot],
            recv_sem=best_recv.at[me],
            device_id={"store": tile},
        )

    def score(place, unit):
        start = pl.multiple_of(place * ny * rows + unit * UNIT, UNIT)
        column = (place * ny * rows) // SUB + unit * (UNIT // SUB)

        @pl.loop(0, stored // group)
        def _(g):
            first = pl.multiple_of(g * group, group)
            picked = blocks[pl.ds(first, group)].reshape(group * width, depth)
            products = lax.dot_general(
                picked,
                gathered[pl.ds(start, UNIT)],
                (((1,), (1,)), ((), ())),
                preferred_element_type=jnp.float32,
            ).reshape(group, width, UNIT)
            factor = scale[pl.ds(first, group)]
            for j in range(UNIT // SUB):
                piece = products[:, :, j * SUB : (j + 1) * SUB] * factor
                best_out[column + j, pl.ds(first, group)] = jnp.max(piece, axis=1)

    def score_and_send(place, unit):
        score(place, unit)
        slot = place * ny
        if unit == 0:
            @pl.when(place != z)
            def _():
                best_copy(slot, 0, 2).start()
        elif unit == 1:
            @pl.when(place != z)
            def _():
                best_copy(slot, 2, 1).start()

            best_copy(slot + 1, 0, 1).start()
        else:
            best_copy(slot + 1, 1, 2).start()

    def each_side(distance, act):
        @pl.loop(0, 2)
        def _(side):
            place = z + (1 - 2 * side) * distance

            @pl.when((place >= 0) & (place < nz) & ((distance > 0) | (side == 0)))
            def _():
                act(place)

    def spread(place, slot, c):
        @pl.when((place >= z) & (z > 0))
        def _():
            copy_of(slot, c, DOWN).start()

        @pl.when((place <= z) & (z < nz - 1))
        def _():
            copy_of(slot, c, UP).start()

    def pass_line(distance, which):
        for c in which:
            def act(place):
                wait_chunk(place * ny, c)
                spread(place, place * ny, c)
                if c < last:
                    copy_of(place * ny, c, ACROSS).start()

            each_side(distance, act)

    def pass_second(distance):
        def act(place):
            wait_chunk(place * ny + 1, last)
            spread(place, place * ny + 1, last)

        each_side(distance, act)

    def across_unit(distance, unit):
        def act(place):
            for c in (0, 1) if unit == 1 else (2, 3, 4):
                wait_chunk(place * ny + 1, c)
            score_and_send(place, unit)

        each_side(distance, act)

    load_own.wait()
    score_and_send(z, 0)

    @pl.loop(1, nz)
    def _(distance):
        pass_second(distance - 1)
        pass_line(distance, (0,))
        across_unit(distance - 1, 1)
        pass_line(distance, (1, 2))
        across_unit(distance - 1, 2)
        pass_line(distance, (3,))
        each_side(distance, lambda place: score_and_send(place, 0))
        pass_line(distance, (4, 5))

    across_unit(nz - 1, 1)
    pass_second(nz - 1)
    across_unit(nz - 1, 2)
    keep = pltpu.make_async_copy(
        best_out.at[pl.ds(mine * subs, subs)], best_in.at[pl.ds(me * subs, subs)], local_sem.at[0]
    )
    keep.start()

    for copy in metas:
        copy.wait()
    for copy in own_meta:
        copy.wait()
    other_meta = [
        pltpu.make_async_copy(src, dst.at[1], smem_sem.at[i])
        for i, (src, dst) in enumerate(
            [(owner_v, owner_s), (block_v, block_s), (pattern_v, pattern_s), (slot_v, slot_s)]
        )
    ]
    for copy in other_meta:
        copy.start()
    for copy in other_meta:
        copy.wait()

    keep.wait()

    @pl.loop(1, n)
    def _(step):
        source = lax.rem(me + step, n)
        pltpu.make_async_remote_copy(
            src_ref=best_out.at[pl.ds(source * subs, subs)],
            dst_ref=best_in.at[pl.ds(source * subs, subs)],
            send_sem=best_send.at[source],
            recv_sem=best_recv.at[source],
            device_id={"store": source},
        ).wait_recv()

    length = owner_s.shape[2]
    slots = lax.broadcasted_iota(jnp.int32, (SLOTS, SUB), 0)

    def merge(c, totals):
        totals = list(totals)
        for run in range(2):
            shard, block = owner_s[run, 0, c], block_s[run, 0, c]
            slot = slot_s[run, 0, c]
            for j in range(subs):
                live = pattern_s[run, 0, c, core * subs + j] == 1
                wanted = jnp.where(live, slot, -1)
                row = best_in[shard * subs + j, pl.ds(block, 1), :]
                piece = jnp.broadcast_to(row, (SLOTS, SUB))
                totals[j] = jnp.maximum(totals[j], jnp.where(slots == wanted, piece, 0.0))
        return tuple(totals)

    zero = jnp.zeros((SLOTS, SUB), jnp.float32)
    totals = lax.fori_loop(0, length, merge, (zero,) * subs)
    for j in range(subs):
        out_ref[0, :, j * SUB : (j + 1) * SUB] = totals[j]

    for c in range(last + 1):
        copy_of(mine, c, ACROSS, True).wait_send()

    @pl.loop(0, nz)
    def _(place):
        slot = place * ny

        @pl.when(place != z)
        def _():
            for c in range(last):
                copy_of(slot, c, ACROSS).wait_send()

        @pl.when((place <= z) & (z < nz - 1))
        def _():
            for c in range(last + 1):
                copy_of(slot, c, UP).wait_send()
            copy_of(slot + 1, last, UP).wait_send()

        @pl.when((place >= z) & (z > 0))
        def _():
            for c in range(last + 1):
                copy_of(slot, c, DOWN).wait_send()
            copy_of(slot + 1, last, DOWN).wait_send()

    @pl.loop(1, n)
    def _(step):
        best_copy(lax.rem(mine + step, n), 0, subs).wait_send()


def body(queries, store_blocks, cand_owner, cand_block, pattern, slot_index):
    n = lax.axis_size("store")
    rows, depth = queries.shape[1:]
    stored, width = store_blocks.shape[:2]
    length, subs = pattern.shape[1:]
    flat = (1, length)
    return pl.pallas_call(
        functools.partial(kernel, n, 16),
        out_shape=jax.ShapeDtypeStruct((1, SLOTS, rows), jnp.float32),
        in_specs=[pl.BlockSpec(memory_space=pl.ANY)] * 6,
        out_specs=pl.BlockSpec(memory_space=pltpu.VMEM),
        scratch_shapes=[
            pltpu.VMEM((stored, width, depth), jnp.bfloat16),
            pltpu.VMEM((n * rows, depth), jnp.bfloat16),
            pltpu.VMEM((stored, width, SUB), jnp.float32),
            pltpu.VMEM((n * rows // SUB, stored, SUB), jnp.float32),
            pltpu.VMEM((n * rows // SUB, stored, SUB), jnp.float32),
            pltpu.VMEM(flat, jnp.int32),
            pltpu.VMEM(flat, jnp.int32),
            pltpu.VMEM((1, length, subs), jnp.int32),
            pltpu.VMEM(flat, jnp.int32),
            pltpu.SMEM((2,) + flat, jnp.int32),
            pltpu.SMEM((2,) + flat, jnp.int32),
            pltpu.SMEM((2, 1, length, subs), jnp.int32),
            pltpu.SMEM((2,) + flat, jnp.int32),
            pltpu.SemaphoreType.DMA((2,)),
            pltpu.SemaphoreType.DMA((n, CHUNKS)),
            pltpu.SemaphoreType.DMA((3, n, CHUNKS)),
            pltpu.SemaphoreType.DMA((n,)),
            pltpu.SemaphoreType.DMA((n,)),
            pltpu.SemaphoreType.DMA((4,)),
            pltpu.SemaphoreType.DMA((4,)),
            pltpu.SemaphoreType.DMA((4,)),
        ],
        compiler_params=pltpu.CompilerParams(
            collective_id=0, has_side_effects=True, vmem_limit_bytes=60 * MIB
        ),
        cost_estimate=pl.CostEstimate(
            flops=2 * n * rows * stored * width * depth,
            bytes_accessed=stored * width * depth * 2,
            transcendentals=0,
        ),
    )(queries, store_blocks, cand_owner, cand_block, pattern, slot_index)


def solution(mesh):
    placed = (
        P(("parts", "store"), "query", None),
        P(("parts", "store"), None, None),
        P(("parts", "store"), "query"),
        P(("parts", "store"), "query"),
        P(("parts", "store"), "query", None),
        P(("parts", "store"), "query"),
    )
    return jax.shard_map(
        body,
        mesh=mesh,
        in_specs=placed,
        out_specs=P(("parts", "store"), None, "query"),
        check_vma=False,
    )
```

```python
import functools
import math

import jax
import jax.numpy as jnp
from jax import lax
from jax.experimental import pallas as pl
from jax.experimental.pallas import tpu as pltpu
from jax.sharding import PartitionSpec as P

SUB = 128
SLOTS = 32
MIB = 1024 * 1024


CHUNKS = 6
UNIT = 256


def kernel(
    n,
    group,
    q_hbm,
    blocks_hbm,
    owner_hbm,
    block_hbm,
    pattern_hbm,
    slot_hbm,
    out_ref,
    blocks,
    gathered,
    scale,
    best_out,
    best_in,
    owner_v,
    block_v,
    pattern_v,
    slot_v,
    owner_s,
    block_s,
    pattern_s,
    slot_s,
    local_sem,
    recv_sem,
    send_sem,
    best_recv,
    best_send,
    meta_recv,
    meta_send,
    smem_sem,
):
    ny = 2
    nz = n // ny
    rows = gathered.shape[0] // n
    small = rows // 6
    sizes = [small] * (CHUNKS - 2) + [2 * small - rows // 8, rows // 8]
    subs = rows // SUB
    stored, width, depth = blocks.shape
    last = CHUNKS - 1
    me = lax.axis_index("store")
    core = lax.axis_index("query")
    y = lax.rem(me, ny)
    z = me // ny
    other_y = 1 - y
    UP, DOWN, ACROSS = 0, 1, 2
    mine = z * ny

    def rows_of(slot, c, count=1):
        start = pl.multiple_of(slot * rows + c * small if c < last else (slot + 1) * rows - sizes[last], 16)
        return gathered.at[pl.ds(start, sum(sizes[c : c + count]))]

    load_blocks = pltpu.make_async_copy(blocks_hbm, blocks, local_sem.at[0])
    load_blocks.start()
    load_own = pltpu.make_async_copy(q_hbm.at[0], rows_of(mine, 0, CHUNKS), local_sem.at[1])
    load_own.start()

    barrier = pltpu.get_barrier_semaphore()

    @pl.loop(1, n)
    def _(step):
        pl.semaphore_signal(barrier, inc=1, device_id={"store": lax.rem(me + step, n)})

    pl.semaphore_signal(barrier, inc=1, device_id={"query": 1 - core})
    pl.semaphore_wait(barrier, n)

    targets = (
        jnp.minimum(z + 1, nz - 1) * ny + y,
        jnp.maximum(z - 1, 0) * ny + y,
        z * ny + other_y,
    )

    def copy_of(slot, c, way, own=False):
        source = q_hbm.at[0, pl.ds(sum(sizes[:c]), sizes[c])] if own else rows_of(slot, c)
        landing = slot + 1 if way == ACROSS else slot
        return pltpu.make_async_remote_copy(
            src_ref=source,
            dst_ref=rows_of(landing, c),
            send_sem=send_sem.at[way, slot, c],
            recv_sem=recv_sem.at[landing, c],
            device_id={"store": targets[way]},
        )

    def wait_chunk(slot, c):
        copy_of(slot, c, UP).wait_recv()

    for c in [last] + list(range(last)):
        copy_of(mine, c, ACROSS, True).start()
    for c in range(last + 1):
        @pl.when(z > 0)
        def _():
            copy_of(mine, c, DOWN, True).start()

        @pl.when(z < nz - 1)
        def _():
            copy_of(mine, c, UP, True).start()

    metas = [
        pltpu.make_async_remote_copy(
            src_ref=src,
            dst_ref=dst,
            send_sem=meta_send.at[i],
            recv_sem=meta_recv.at[i],
            device_id={"query": 1 - core},
        )
        for i, (src, dst) in enumerate(
            [(owner_hbm, owner_v), (block_hbm, block_v), (pattern_hbm, pattern_v), (slot_hbm, slot_v)]
        )
    ]
    for copy in metas:
        copy.start()
    own_meta = [
        pltpu.make_async_copy(src, dst.at[0], smem_sem.at[i])
        for i, (src, dst) in enumerate(
            [(owner_hbm, owner_s), (block_hbm, block_s), (pattern_hbm, pattern_s), (slot_hbm, slot_s)]
        )
    ]
    for copy in own_meta:
        copy.start()

    load_blocks.wait()

    @pl.loop(0, stored)
    def _(b):
        wide = blocks[b].astype(jnp.float32)
        mean = jnp.sum(wide * wide, axis=1, keepdims=True) * (1.0 / depth)
        inverse = lax.rsqrt(mean + 1e-06) * (1.0 / math.sqrt(depth))
        scale[b] = jnp.broadcast_to(inverse, (width, SUB))

    def best_copy(slot, first, count):
        tile = (slot // ny) * ny + lax.rem(slot + y, ny)
        return pltpu.make_async_remote_copy(
            src_ref=best_out.at[pl.ds(slot * subs + first, count)],
            dst_ref=best_in.at[pl.ds(me * subs + first, count)],
            send_sem=best_send.at[slot],
            recv_sem=best_recv.at[me],
            device_id={"store": tile},
        )

    def score(place, unit):
        start = pl.multiple_of(place * ny * rows + unit * UNIT, UNIT)
        column = (place * ny * rows) // SUB + unit * (UNIT // SUB)

        @pl.loop(0, stored // group)
        def _(g):
            first = pl.multiple_of(g * group, group)
            picked = blocks[pl.ds(first, group)].reshape(group * width, depth)
            products = lax.dot_general(
                picked,
                gathered[pl.ds(start, UNIT)],
                (((1,), (1,)), ((), ())),
                preferred_element_type=jnp.float32,
            ).reshape(group, width, UNIT)
            factor = scale[pl.ds(first, group)]
            for j in range(UNIT // SUB):
                piece = products[:, :, j * SUB : (j + 1) * SUB] * factor
                best_out[column + j, pl.ds(first, group)] = jnp.max(piece, axis=1)

    def score_and_send(place, unit):
        score(place, unit)
        slot = place * ny
        if unit == 0:
            @pl.when(place != z)
            def _():
                best_copy(slot, 0, 2).start()
        elif unit == 1:
            @pl.when(place != z)
            def _():
                best_copy(slot, 2, 1).start()

            best_copy(slot + 1, 0, 1).start()
        else:
            best_copy(slot + 1, 1, 2).start()

    def each_side(distance, act):
        @pl.loop(0, 2)
        def _(side):
            place = z + (1 - 2 * side) * distance

            @pl.when((place >= 0) & (place < nz) & ((distance > 0) | (side == 0)))
            def _():
                act(place)

    def spread(place, slot, c):
        @pl.when((place >= z) & (z > 0))
        def _():
            copy_of(slot, c, DOWN).start()

        @pl.when((place <= z) & (z < nz - 1))
        def _():
            copy_of(slot, c, UP).start()

    def pass_line(distance, which):
        for c in which:
            def act(place):
                wait_chunk(place * ny, c)
                spread(place, place * ny, c)
                if c < last:
                    copy_of(place * ny, c, ACROSS).start()

            each_side(distance, act)

    def pass_second(distance):
        def act(place):
            wait_chunk(place * ny + 1, last)
            spread(place, place * ny + 1, last)

        each_side(distance, act)

    def across_unit(distance, unit):
        def act(place):
            for c in (0, 1) if unit == 1 else (2, 3, 4):
                wait_chunk(place * ny + 1, c)
            score_and_send(place, unit)

        each_side(distance, act)

    load_own.wait()
    score_and_send(z, 0)
    for copy in metas:
        copy.wait()
    for copy in own_meta:
        copy.wait()
    other_meta = [
        pltpu.make_async_copy(src, dst.at[1], smem_sem.at[i])
        for i, (src, dst) in enumerate(
            [(owner_v, owner_s), (block_v, block_s), (pattern_v, pattern_s), (slot_v, slot_s)]
        )
    ]
    for copy in other_meta:
        copy.start()

    @pl.loop(1, nz)
    def _(distance):
        pass_second(distance - 1)
        pass_line(distance, (0,))
        across_unit(distance - 1, 1)
        pass_line(distance, (1, 2))
        across_unit(distance - 1, 2)
        pass_line(distance, (3,))
        each_side(distance, lambda place: score_and_send(place, 0))
        pass_line(distance, (4, 5))

    across_unit(nz - 1, 1)
    pass_second(nz - 1)
    across_unit(nz - 1, 2)
    keep = pltpu.make_async_copy(
        best_out.at[pl.ds(mine * subs, subs)], best_in.at[pl.ds(me * subs, subs)], local_sem.at[0]
    )
    keep.start()

    for copy in other_meta:
        copy.wait()

    for c in range(last + 1):
        copy_of(mine, c, ACROSS, True).wait_send()

    @pl.loop(0, nz)
    def _(place):
        slot = place * ny

        @pl.when(place != z)
        def _():
            for c in range(last):
                copy_of(slot, c, ACROSS).wait_send()

        @pl.when((place <= z) & (z < nz - 1))
        def _():
            for c in range(last + 1):
                copy_of(slot, c, UP).wait_send()
            copy_of(slot + 1, last, UP).wait_send()

        @pl.when((place >= z) & (z > 0))
        def _():
            for c in range(last + 1):
                copy_of(slot, c, DOWN).wait_send()
            copy_of(slot + 1, last, DOWN).wait_send()

    keep.wait()

    @pl.loop(1, n)
    def _(step):
        source = lax.rem(me + step, n)
        pltpu.make_async_remote_copy(
            src_ref=best_out.at[pl.ds(source * subs, subs)],
            dst_ref=best_in.at[pl.ds(source * subs, subs)],
            send_sem=best_send.at[source],
            recv_sem=best_recv.at[source],
            device_id={"store": source},
        ).wait_recv()

    length = owner_s.shape[2]
    slots = lax.broadcasted_iota(jnp.int32, (SLOTS, SUB), 0)

    def merge(c, totals):
        totals = list(totals)
        for run in range(2):
            shard, block = owner_s[run, 0, c], block_s[run, 0, c]
            slot = slot_s[run, 0, c]
            for j in range(subs):
                live = pattern_s[run, core * subs + j, 0, c] == 1
                wanted = jnp.where(live, slot, -1)
                row = best_in[shard * subs + j, pl.ds(block, 1), :]
                piece = jnp.broadcast_to(row, (SLOTS, SUB))
                totals[j] = jnp.maximum(totals[j], jnp.where(slots == wanted, piece, 0.0))
        return tuple(totals)

    zero = jnp.zeros((SLOTS, SUB), jnp.float32)
    totals = lax.fori_loop(0, length, merge, (zero,) * subs, unroll=8)
    for j in range(subs):
        out_ref[0, :, j * SUB : (j + 1) * SUB] = totals[j]

    @pl.loop(1, n)
    def _(step):
        best_copy(lax.rem(mine + step, n), 0, subs).wait_send()


def body(queries, store_blocks, cand_owner, cand_block, pattern, slot_index):
    n = lax.axis_size("store")
    rows, depth = queries.shape[1:]
    stored, width = store_blocks.shape[:2]
    length, subs = pattern.shape[1:]
    flat = (1, length)
    return pl.pallas_call(
        functools.partial(kernel, n, 32),
        out_shape=jax.ShapeDtypeStruct((1, SLOTS, rows), jnp.float32),
        in_specs=[pl.BlockSpec(memory_space=pl.ANY)] * 6,
        out_specs=pl.BlockSpec(memory_space=pltpu.VMEM),
        scratch_shapes=[
            pltpu.VMEM((stored, width, depth), jnp.bfloat16),
            pltpu.VMEM((n * rows, depth), jnp.bfloat16),
            pltpu.VMEM((stored, width, SUB), jnp.float32),
            pltpu.VMEM((n * rows // SUB, stored, SUB), jnp.float32),
            pltpu.VMEM((n * rows // SUB, stored, SUB), jnp.float32),
            pltpu.VMEM(flat, jnp.int32),
            pltpu.VMEM(flat, jnp.int32),
            pltpu.VMEM((subs, 1, length), jnp.int32),
            pltpu.VMEM(flat, jnp.int32),
            pltpu.SMEM((2,) + flat, jnp.int32),
            pltpu.SMEM((2,) + flat, jnp.int32),
            pltpu.SMEM((2, subs, 1, length), jnp.int32),
            pltpu.SMEM((2,) + flat, jnp.int32),
            pltpu.SemaphoreType.DMA((2,)),
            pltpu.SemaphoreType.DMA((n, CHUNKS)),
            pltpu.SemaphoreType.DMA((3, n, CHUNKS)),
            pltpu.SemaphoreType.DMA((n,)),
            pltpu.SemaphoreType.DMA((n,)),
            pltpu.SemaphoreType.DMA((4,)),
            pltpu.SemaphoreType.DMA((4,)),
            pltpu.SemaphoreType.DMA((4,)),
        ],
        compiler_params=pltpu.CompilerParams(
            collective_id=0, has_side_effects=True, vmem_limit_bytes=60 * MIB
        ),
        cost_estimate=pl.CostEstimate(
            flops=2 * n * rows * stored * width * depth,
            bytes_accessed=stored * width * depth * 2,
            transcendentals=0,
        ),
    )(queries, store_blocks, cand_owner, cand_block, pattern.transpose(2, 0, 1), slot_index)


def solution(mesh):
    placed = (
        P(("parts", "store"), "query", None),
        P(("parts", "store"), None, None),
        P(("parts", "store"), "query"),
        P(("parts", "store"), "query"),
        P(("parts", "store"), "query", None),
        P(("parts", "store"), "query"),
    )
    return jax.shard_map(
        body,
        mesh=mesh,
        in_specs=placed,
        out_specs=P(("parts", "store"), None, "query"),
        check_vma=False,
    )
```

```python
import functools
import math

import jax
import jax.numpy as jnp
from jax import lax
from jax.experimental import pallas as pl
from jax.experimental.pallas import tpu as pltpu
from jax.sharding import PartitionSpec as P

SUB = 128
SLOTS = 32
MIB = 1024 * 1024


CHUNKS = 6
UNIT = 256


def kernel(
    n,
    group,
    q_hbm,
    blocks_hbm,
    owner_hbm,
    block_hbm,
    pattern_hbm,
    slot_hbm,
    out_ref,
    blocks,
    gathered,
    scale,
    best_out,
    best_in,
    owner_v,
    block_v,
    pattern_v,
    slot_v,
    owner_s,
    block_s,
    pattern_s,
    slot_s,
    local_sem,
    recv_sem,
    send_sem,
    best_recv,
    best_send,
    meta_recv,
    meta_send,
    smem_sem,
):
    ny = 2
    nz = n // ny
    rows = gathered.shape[0] // n
    small = rows // 6
    sizes = [small] * (CHUNKS - 2) + [2 * small - rows // 6, rows // 6]
    subs = rows // SUB
    stored, width, depth = blocks.shape
    last = CHUNKS - 1
    me = lax.axis_index("store")
    core = lax.axis_index("query")
    y = lax.rem(me, ny)
    z = me // ny
    other_y = 1 - y
    UP, DOWN, ACROSS = 0, 1, 2
    mine = z * ny

    def rows_of(slot, c, count=1):
        start = pl.multiple_of(slot * rows + c * small if c < last else (slot + 1) * rows - sizes[last], 16)
        return gathered.at[pl.ds(start, sum(sizes[c : c + count]))]

    load_blocks = pltpu.make_async_copy(blocks_hbm, blocks, local_sem.at[0])
    load_blocks.start()
    load_own = pltpu.make_async_copy(q_hbm.at[0], rows_of(mine, 0, CHUNKS), local_sem.at[1])
    load_own.start()

    barrier = pltpu.get_barrier_semaphore()

    @pl.loop(1, n)
    def _(step):
        pl.semaphore_signal(barrier, inc=1, device_id={"store": lax.rem(me + step, n)})

    pl.semaphore_signal(barrier, inc=1, device_id={"query": 1 - core})
    pl.semaphore_wait(barrier, n)

    targets = (
        jnp.minimum(z + 1, nz - 1) * ny + y,
        jnp.maximum(z - 1, 0) * ny + y,
        z * ny + other_y,
    )

    def copy_of(slot, c, way, own=False):
        source = q_hbm.at[0, pl.ds(sum(sizes[:c]), sizes[c])] if own else rows_of(slot, c)
        landing = slot + 1 if way == ACROSS else slot
        return pltpu.make_async_remote_copy(
            src_ref=source,
            dst_ref=rows_of(landing, c),
            send_sem=send_sem.at[way, slot, c],
            recv_sem=recv_sem.at[landing, c],
            device_id={"store": targets[way]},
        )

    def wait_chunk(slot, c):
        copy_of(slot, c, UP).wait_recv()

    for c in [last] + list(range(last)):
        copy_of(mine, c, ACROSS, True).start()
    for c in range(last + 1):
        @pl.when(z > 0)
        def _():
            copy_of(mine, c, DOWN, True).start()

        @pl.when(z < nz - 1)
        def _():
            copy_of(mine, c, UP, True).start()

    metas = [
        pltpu.make_async_remote_copy(
            src_ref=src,
            dst_ref=dst,
            send_sem=meta_send.at[i],
            recv_sem=meta_recv.at[i],
            device_id={"query": 1 - core},
        )
        for i, (src, dst) in enumerate(
            [(owner_hbm, owner_v), (block_hbm, block_v), (pattern_hbm, pattern_v), (slot_hbm, slot_v)]
        )
    ]
    for copy in metas:
        copy.start()
    own_meta = [
        pltpu.make_async_copy(src, dst.at[0], smem_sem.at[i])
        for i, (src, dst) in enumerate(
            [(owner_hbm, owner_s), (block_hbm, block_s), (pattern_hbm, pattern_s), (slot_hbm, slot_s)]
        )
    ]
    for copy in own_meta:
        copy.start()

    load_blocks.wait()

    @pl.loop(0, stored)
    def _(b):
        wide = blocks[b].astype(jnp.float32)
        mean = jnp.sum(wide * wide, axis=1, keepdims=True) * (1.0 / depth)
        inverse = lax.rsqrt(mean + 1e-06) * (1.0 / math.sqrt(depth))
        scale[b] = jnp.broadcast_to(inverse, (width, SUB))

    def best_copy(slot, first, count):
        tile = (slot // ny) * ny + lax.rem(slot + y, ny)
        return pltpu.make_async_remote_copy(
            src_ref=best_out.at[pl.ds(slot * subs + first, count)],
            dst_ref=best_in.at[pl.ds(me * subs + first, count)],
            send_sem=best_send.at[slot],
            recv_sem=best_recv.at[me],
            device_id={"store": tile},
        )

    def score(place, unit):
        start = pl.multiple_of(place * ny * rows + unit * UNIT, UNIT)
        column = (place * ny * rows) // SUB + unit * (UNIT // SUB)

        @pl.loop(0, stored // group)
        def _(g):
            first = pl.multiple_of(g * group, group)
            picked = blocks[pl.ds(first, group)].reshape(group * width, depth)
            products = lax.dot_general(
                picked,
                gathered[pl.ds(start, UNIT)],
                (((1,), (1,)), ((), ())),
                preferred_element_type=jnp.float32,
            ).reshape(group, width, UNIT)
            factor = scale[pl.ds(first, group)]
            for j in range(UNIT // SUB):
                piece = products[:, :, j * SUB : (j + 1) * SUB] * factor
                best_out[column + j, pl.ds(first, group)] = jnp.max(piece, axis=1)

    def score_and_send(place, unit):
        score(place, unit)
        slot = place * ny
        if unit == 0:
            @pl.when(place != z)
            def _():
                best_copy(slot, 0, 2).start()
        elif unit == 1:
            @pl.when(place != z)
            def _():
                best_copy(slot, 2, 1).start()

            best_copy(slot + 1, 0, 1).start()
        else:
            best_copy(slot + 1, 1, 2).start()

    def each_side(distance, act):
        @pl.loop(0, 2)
        def _(side):
            place = z + (1 - 2 * side) * distance

            @pl.when((place >= 0) & (place < nz) & ((distance > 0) | (side == 0)))
            def _():
                act(place)

    def spread(place, slot, c):
        @pl.when((place >= z) & (z > 0))
        def _():
            copy_of(slot, c, DOWN).start()

        @pl.when((place <= z) & (z < nz - 1))
        def _():
            copy_of(slot, c, UP).start()

    def pass_line(distance, which):
        for c in which:
            def act(place):
                wait_chunk(place * ny, c)
                spread(place, place * ny, c)
                if c < last:
                    copy_of(place * ny, c, ACROSS).start()

            each_side(distance, act)

    def pass_second(distance):
        def act(place):
            wait_chunk(place * ny + 1, last)
            spread(place, place * ny + 1, last)

        each_side(distance, act)

    def across_unit(distance, unit):
        def act(place):
            for c in (0, 1) if unit == 1 else (2, 3, 4):
                wait_chunk(place * ny + 1, c)
            score_and_send(place, unit)

        each_side(distance, act)

    load_own.wait()
    score_and_send(z, 0)
    for copy in metas:
        copy.wait()
    for copy in own_meta:
        copy.wait()
    other_meta = [
        pltpu.make_async_copy(src, dst.at[1], smem_sem.at[i])
        for i, (src, dst) in enumerate(
            [(owner_v, owner_s), (block_v, block_s), (pattern_v, pattern_s), (slot_v, slot_s)]
        )
    ]
    for copy in other_meta:
        copy.start()

    @pl.loop(1, nz)
    def _(distance):
        pass_second(distance - 1)
        pass_line(distance, (0, 1))
        across_unit(distance - 1, 1)
        pass_line(distance, (2, 3))
        across_unit(distance - 1, 2)
        each_side(distance, lambda place: score_and_send(place, 0))
        pass_line(distance, (4, 5))

    across_unit(nz - 1, 1)
    pass_second(nz - 1)
    across_unit(nz - 1, 2)
    keep = pltpu.make_async_copy(
        best_out.at[pl.ds(mine * subs, subs)], best_in.at[pl.ds(me * subs, subs)], local_sem.at[0]
    )
    keep.start()

    for copy in other_meta:
        copy.wait()

    for c in range(last + 1):
        copy_of(mine, c, ACROSS, True).wait_send()

    @pl.loop(0, nz)
    def _(place):
        slot = place * ny

        @pl.when(place != z)
        def _():
            for c in range(last):
                copy_of(slot, c, ACROSS).wait_send()

        @pl.when((place <= z) & (z < nz - 1))
        def _():
            for c in range(last + 1):
                copy_of(slot, c, UP).wait_send()
            copy_of(slot + 1, last, UP).wait_send()

        @pl.when((place >= z) & (z > 0))
        def _():
            for c in range(last + 1):
                copy_of(slot, c, DOWN).wait_send()
            copy_of(slot + 1, last, DOWN).wait_send()

    keep.wait()

    @pl.loop(1, n)
    def _(step):
        source = lax.rem(me + step, n)
        pltpu.make_async_remote_copy(
            src_ref=best_out.at[pl.ds(source * subs, subs)],
            dst_ref=best_in.at[pl.ds(source * subs, subs)],
            send_sem=best_send.at[source],
            recv_sem=best_recv.at[source],
            device_id={"store": source},
        ).wait_recv()

    length = owner_s.shape[2]
    slots = lax.broadcasted_iota(jnp.int32, (SLOTS, SUB), 0)

    def merge(c, totals):
        totals = list(totals)
        for run in range(2):
            shard, block = owner_s[run, 0, c], block_s[run, 0, c]
            slot = slot_s[run, 0, c]
            for j in range(subs):
                live = pattern_s[run, core * subs + j, 0, c] == 1
                wanted = jnp.where(live, slot, -1)
                row = best_in[shard * subs + j, pl.ds(block, 1), :]
                piece = jnp.broadcast_to(row, (SLOTS, SUB))
                totals[j] = jnp.maximum(totals[j], jnp.where(slots == wanted, piece, 0.0))
        return tuple(totals)

    zero = jnp.zeros((SLOTS, SUB), jnp.float32)
    totals = lax.fori_loop(0, length, merge, (zero,) * subs, unroll=8)
    for j in range(subs):
        out_ref[0, :, j * SUB : (j + 1) * SUB] = totals[j]

    @pl.loop(1, n)
    def _(step):
        best_copy(lax.rem(mine + step, n), 0, subs).wait_send()


def body(queries, store_blocks, cand_owner, cand_block, pattern, slot_index):
    n = lax.axis_size("store")
    rows, depth = queries.shape[1:]
    stored, width = store_blocks.shape[:2]
    length, subs = pattern.shape[1:]
    flat = (1, length)
    return pl.pallas_call(
        functools.partial(kernel, n, 32),
        out_shape=jax.ShapeDtypeStruct((1, SLOTS, rows), jnp.float32),
        in_specs=[pl.BlockSpec(memory_space=pl.ANY)] * 6,
        out_specs=pl.BlockSpec(memory_space=pltpu.VMEM),
        scratch_shapes=[
            pltpu.VMEM((stored, width, depth), jnp.bfloat16),
            pltpu.VMEM((n * rows, depth), jnp.bfloat16),
            pltpu.VMEM((stored, width, SUB), jnp.float32),
            pltpu.VMEM((n * rows // SUB, stored, SUB), jnp.float32),
            pltpu.VMEM((n * rows // SUB, stored, SUB), jnp.float32),
            pltpu.VMEM(flat, jnp.int32),
            pltpu.VMEM(flat, jnp.int32),
            pltpu.VMEM((subs, 1, length), jnp.int32),
            pltpu.VMEM(flat, jnp.int32),
            pltpu.SMEM((2,) + flat, jnp.int32),
            pltpu.SMEM((2,) + flat, jnp.int32),
            pltpu.SMEM((2, subs, 1, length), jnp.int32),
            pltpu.SMEM((2,) + flat, jnp.int32),
            pltpu.SemaphoreType.DMA((2,)),
            pltpu.SemaphoreType.DMA((n, CHUNKS)),
            pltpu.SemaphoreType.DMA((3, n, CHUNKS)),
            pltpu.SemaphoreType.DMA((n,)),
            pltpu.SemaphoreType.DMA((n,)),
            pltpu.SemaphoreType.DMA((4,)),
            pltpu.SemaphoreType.DMA((4,)),
            pltpu.SemaphoreType.DMA((4,)),
        ],
        compiler_params=pltpu.CompilerParams(
            collective_id=0, has_side_effects=True, vmem_limit_bytes=60 * MIB
        ),
        cost_estimate=pl.CostEstimate(
            flops=2 * n * rows * stored * width * depth,
            bytes_accessed=stored * width * depth * 2,
            transcendentals=0,
        ),
    )(queries, store_blocks, cand_owner, cand_block, pattern.transpose(2, 0, 1), slot_index)


def solution(mesh):
    placed = (
        P(("parts", "store"), "query", None),
        P(("parts", "store"), None, None),
        P(("parts", "store"), "query"),
        P(("parts", "store"), "query"),
        P(("parts", "store"), "query", None),
        P(("parts", "store"), "query"),
    )
    return jax.shard_map(
        body,
        mesh=mesh,
        in_specs=placed,
        out_specs=P(("parts", "store"), None, "query"),
        check_vma=False,
    )
```
